32 devices in a mesh: ctx: 8 (over z, core), tp: 4 (over y, x).
Axes of the slice: x: 2, y: 2, z: 4, core: 2. Of those that a mesh axis runs over, the one named last changes fastest.
Arguments:
- query_field: bfloat16 [8192, 4096], P('ctx', 'tp'), may hold values from -6 to 6
- key_field: bfloat16 [8192, 4096], P('ctx', 'tp'), may hold values from -6 to 6
- value_field: bfloat16 [8192, 4096], P('ctx', 'tp'), may hold values from -6 to 6
- upstream: bfloat16 [8192, 4096], P('ctx', 'tp'), may hold values from -6 to 6
- decay_rates: float32 [16, 4096], P(None, 'tp'), may hold values from 6.1035156e-05 to 0.05
- frequencies: float32 [16, 4096], P(None, 'tp'), may hold values from 0 to 1
- residues: float32 [16, 4096], P(None, 'tp'), may hold values from -1.5 to 1.5
- passthrough: float32 [4096], P('tp'), may hold values from 0.5 to 1.5
- norm_gain: float32 [4096], P('tp'), may hold values from 0.5 to 1.5
Outputs:
- output: bfloat16 [8192, 4096], P('ctx', 'tp')
- grad_queries: bfloat16 [8192, 4096], P('ctx', 'tp')
- grad_keys: bfloat16 [8192, 4096], P('ctx', 'tp')
- grad_values: bfloat16 [8192, 4096], P('ctx', 'tp')
- grad_gain: float32 [4096], P('tp')
The draws below stay inside these ranges and needn't reach their ends.
All inputs are finite; a program needn't handle non-finite values.
Results may differ from the reference program's by a relative error of at most 0.01.
Values may be sent and summed in bfloat16 or wider, within the bound.
A program may use at most 192 MiB of HBM per device.

```python
import math
import jax
import jax.numpy as jnp
from jax import lax

D = 4096
MODES = 16
LENGTH = 8192


def steps_of(own_key, shape, shards, least, high):
    def one(dim, blocks):
        heights = jax.random.uniform(jax.random.fold_in(jax.random.fold_in(own_key, 6), dim), (blocks,), jnp.float32, least / len(shards), high / len(shards))
        return jnp.repeat(jnp.exp(heights), shape[dim] // blocks).reshape((-1,) + (1,) * (len(shape) - dim - 1))

    level = one(*shards[0])
    for cut in shards[1:]:
        level = level * one(*cut)
    return level


def scatter_about(stream_key, dims, width, limit, pieces=(), kind=jnp.bfloat16):
    values = width * jax.random.normal(stream_key, dims, jnp.float32)
    if pieces:
        values = values * steps_of(stream_key, dims, pieces, -0.22, 0.18)
    return jnp.clip(values, -limit, limit).astype(kind)


def setup_inputs(seed: int = 0) -> dict:
    seeds = jax.random.split(jax.random.key(seed), 10)
    return {
        "query_field": scatter_about(seeds[0], (LENGTH, D), 1.0, 6.0, ((0, 8), (1, 4))),
        "key_field": scatter_about(seeds[1], (LENGTH, D), 1.0, 6.0, ((0, 8), (1, 4))),
        "value_field": scatter_about(seeds[2], (LENGTH, D), 1.0, 6.0, ((0, 8), (1, 4))),
        "upstream": scatter_about(seeds[3], (LENGTH, D), 1.0, 6.0, ((0, 8), (1, 4))),
        "decay_rates": jnp.clip(jnp.exp(math.log(0.05) - 6.7083283 * jax.random.uniform(seeds[4], (MODES, D), jnp.float32) ** steps_of(seeds[4], (MODES, D), ((1, 4),), -0.2, 0.2)), 6.103515625e-05, 0.05),
        "frequencies": jnp.clip(1.0 * jax.random.uniform(seeds[5], (MODES, D), jnp.float32) ** steps_of(seeds[5], (MODES, D), ((1, 4),), -0.2, 0.2), 0.0, 1.0),
        "residues": scatter_about(seeds[6], (MODES, D), MODES ** -0.5, 1.5, ((1, 4),), jnp.float32),
        "passthrough": jnp.clip(0.5 + 1.0 * jax.random.uniform(seeds[7], (D,), jnp.float32) ** steps_of(seeds[7], (D,), ((0, 4),), -0.2, 0.2), 0.5, 1.5),
        "norm_gain": jnp.clip(1.0 + 0.1 * jax.random.normal(seeds[8], (D,), jnp.float32), 0.5, 1.5),
    }


def modal_filter(decay_rates, frequencies, residues, length):
    positions = jnp.arange(length, dtype=jnp.float32)
    filter_taps = jnp.zeros((decay_rates.shape[1], length), jnp.float32)
    for mode_index in range(decay_rates.shape[0]):
        rate_col = decay_rates[mode_index][:, None]
        freq_col = frequencies[mode_index][:, None]
        residue_col = residues[mode_index][:, None]
        filter_taps = filter_taps + residue_col * jnp.sqrt(rate_col) * jnp.exp(-rate_col * positions) * jnp.cos(freq_col * positions)
    return filter_taps

def reference(query_field, key_field, value_field, upstream, decay_rates, frequencies, residues, passthrough, norm_gain):
    length = query_field.shape[0]
    channels = query_field.shape[1]
    block_size = min(256, channels)
    block_count = channels // block_size
    points = 2 * length
    product_field = (key_field.astype(jnp.float32) * value_field.astype(jnp.float32)).astype(jnp.bfloat16)

    def to_blocks(array):
        return array.T.reshape(block_count, block_size, length)

    def param_blocks(param):
        return param.reshape(param.shape[0], block_count, block_size).transpose(1, 0, 2)

    def from_blocks(array):
        return array.reshape(channels, length).T
    params = (param_blocks(decay_rates), param_blocks(frequencies), param_blocks(residues), passthrough.reshape(block_count, block_size))

    def conv_block(inputs):
        signal, rate_blk, freq_blk, residue_blk, skip_blk = inputs
        taps_spec = jnp.fft.rfft(modal_filter(rate_blk, freq_blk, residue_blk, length), n=points, axis=-1)
        signal_f = signal.astype(jnp.float32)
        sig_spec = jnp.fft.rfft(signal_f, n=points, axis=-1)
        result = jnp.fft.irfft(taps_spec * sig_spec, n=points, axis=-1)[:, :length]
        return (result + skip_blk[:, None] * signal_f).astype(jnp.bfloat16)

    def corr_block(inputs):
        signal, rate_blk, freq_blk, residue_blk, skip_blk = inputs
        taps_spec = jnp.fft.rfft(modal_filter(rate_blk, freq_blk, residue_blk, length), n=points, axis=-1)
        signal_f = signal.astype(jnp.float32)
        sig_spec = jnp.fft.rfft(signal_f, n=points, axis=-1)
        result = jnp.fft.irfft(jnp.conj(taps_spec) * sig_spec, n=points, axis=-1)[:, :length]
        return (result + skip_blk[:, None] * signal_f).astype(jnp.bfloat16)
    conv_out = from_blocks(lax.map(conv_block, (to_blocks(product_field),) + params))
    gated = query_field.astype(jnp.float32) * conv_out.astype(jnp.float32)
    scale = lax.rsqrt(lax.optimization_barrier(jnp.sum(gated * gated, axis=1)) / channels + 1e-06)[:, None]
    normed = gated * scale
    output = (normed * norm_gain).astype(jnp.bfloat16)
    upstream_f = upstream.astype(jnp.float32)
    grad_in = upstream_f * norm_gain
    inner_prod = lax.optimization_barrier(jnp.sum(grad_in * normed, axis=1)) / channels
    grad_gated = scale * (grad_in - normed * inner_prod[:, None])
    grad_gain = lax.optimization_barrier(jnp.sum(upstream_f * normed, axis=0))
    grad_queries = (grad_gated * conv_out.astype(jnp.float32)).astype(jnp.bfloat16)
    grad_conv = (grad_gated * query_field.astype(jnp.float32)).astype(jnp.bfloat16)
    grad_field = from_blocks(lax.map(corr_block, (to_blocks(grad_conv),) + params)).astype(jnp.float32)
    grad_keys = (grad_field * value_field.astype(jnp.float32)).astype(jnp.bfloat16)
    grad_values = (grad_field * key_field.astype(jnp.float32)).astype(jnp.bfloat16)
    return (output, grad_queries, grad_keys, grad_values, grad_gain)
```

```python
import functools

import jax
import jax.numpy as jnp
from jax import lax
from jax.experimental import pallas as pl
from jax.experimental.pallas import tpu as pltpu
from jax.sharding import PartitionSpec as P

D = 4096
EPS = 1e-06
B = 16
LANES = 128
F32 = jnp.float32
BF16 = jnp.bfloat16


def permute_in(x, nat, perm, chunks):
    nat[...] = x
    for b in range(B):
        perm[pl.ds(b * chunks, chunks), :] = nat[pl.ds(b, chunks, stride=B), :]


def chunk_states(perm, powers, states, modes, chunks, forward):
    def step(i, carry):
        total = [[jnp.zeros((chunks, LANES), F32) for _ in range(2)] for _ in range(2)]
        for b in range(B):
            x = perm[pl.ds(b * chunks, chunks), :]
            k = B - b if forward else b + 1
            for j in range(2):
                m = 2 * i + j
                total[j][0] = total[j][0] + powers[m, k : k + 1, :] * x
                total[j][1] = total[j][1] + powers[m, B + 1 + k : B + 2 + k, :] * x
        for j in range(2):
            for part in range(2):
                row = pl.multiple_of((part * modes + 2 * i + j) * chunks, 8)
                states[pl.ds(row, chunks), :] = total[j][part]
        return carry

    lax.fori_loop(0, modes // 2, step, 0)


def scan_chunks(states, first_re, first_im, powers_re, powers_im, out, modes, chunks, forward):
    def step(n, carry):
        re, im = carry
        a = n if forward else chunks - 1 - n
        at_re = pl.ds(a, modes, stride=chunks)
        at_im = pl.ds(modes * chunks + a, modes, stride=chunks)
        own_re = states[at_re, :]
        own_im = states[at_im, :]
        if out is not None:
            out[at_re, :] = re
            out[at_im, :] = im
        return (
            powers_re * re - powers_im * im + own_re,
            powers_re * im + powers_im * re + own_im,
        )

    return lax.fori_loop(0, chunks, step, (first_re, first_im), unroll=4)


def expand(perm, incoming, taps, gains, result, modes, chunks, forward):
    width = 4
    for g in range(B // width):
        rows = [g * width + j for j in range(width)]
        total = [None] * width
        for s in range(B):
            lags = [(t - s if forward else s - t) for t in rows]
            if max(lags) < 0:
                continue
            x = perm[pl.ds(s * chunks, chunks), :]
            for j, lag in enumerate(lags):
                if lag >= 0:
                    term = taps[lag : lag + 1, :] * x
                    total[j] = term if total[j] is None else total[j] + term

        def step(i, carry):
            carry = list(carry)
            for h in range(2):
                m = 2 * i + h
                re = incoming[pl.ds(pl.multiple_of(m * chunks, 8), chunks), :]
                im = incoming[pl.ds(pl.multiple_of((modes + m) * chunks, 8), chunks), :]
                for j, t in enumerate(rows):
                    k = t if forward else B - 1 - t
                    carry[j] = (
                        carry[j] + gains[m, k : k + 1, :] * re + gains[m, B + k : B + k + 1, :] * im
                    )
            return tuple(carry)

        total = lax.fori_loop(0, modes // 2, step, tuple(total))
        for j, t in enumerate(rows):
            result[pl.ds(t, chunks, stride=B), :] = total[j]


def forward_states_kernel(modes, chunks, key, value, powers, jump, states, last, nat, perm):
    field = (key[...].astype(F32) * value[...].astype(F32)).astype(BF16).astype(F32)
    permute_in(field, nat, perm, chunks)
    chunk_states(perm, powers, states, modes, chunks, True)
    zero = jnp.zeros((modes, LANES), F32)
    re, im = scan_chunks(states, zero, zero, jump[0], jump[1], None, modes, chunks, True)
    last[0] = re
    last[1] = im


def forward_kernel(
    modes, chunks, key, value, query, up, gain, states, first, jump, taps, gains,
    conv, squares, inners, nat, perm, incoming,
):
    field = (key[...].astype(F32) * value[...].astype(F32)).astype(BF16).astype(F32)
    permute_in(field, nat, perm, chunks)
    scan_chunks(states, first[0], first[1], jump[0], jump[1], incoming, modes, chunks, True)
    expand(perm, incoming, taps, gains, nat, modes, chunks, True)
    conv_out = nat[...].astype(BF16)
    conv[...] = conv_out
    gated = query[...].astype(F32) * conv_out.astype(F32)

    @pl.when(pl.program_id(0) == 0)
    def _():
        squares[...] = jnp.zeros_like(squares)
        inners[...] = jnp.zeros_like(inners)

    squares[...] += gated * gated
    inners[...] += up[...].astype(F32) * gain[...] * gated


def middle_kernel(
    modes, chunks, query, up, conv, gain, scale, inner, powers, jump,
    output, query_grad, conv_grad, gain_grad, states, last, nat, perm,
):
    q = query[...].astype(F32)
    c = conv[...].astype(F32)
    u = up[...].astype(F32)
    s = scale[...]
    normed = q * c * s
    output[...] = (normed * gain[...]).astype(BF16)
    gain_grad[...] = jnp.sum(u * normed, axis=0, keepdims=True)
    grad_gated = s * (u * gain[...] - normed * inner[...])
    query_grad[...] = (grad_gated * c).astype(BF16)
    w = (grad_gated * q).astype(BF16)
    conv_grad[...] = w
    permute_in(w.astype(F32), nat, perm, chunks)
    chunk_states(perm, powers, states, modes, chunks, False)
    zero = jnp.zeros((modes, LANES), F32)
    re, im = scan_chunks(states, zero, zero, jump[0], jump[1], None, modes, chunks, False)
    last[0] = re
    last[1] = im


def backward_kernel(
    modes, chunks, conv_grad, key, value, states, first, jump, taps, gains,
    key_grad, value_grad, nat, perm, incoming,
):
    permute_in(conv_grad[...].astype(F32), nat, perm, chunks)
    scan_chunks(states, first[0], first[1], jump[0], jump[1], incoming, modes, chunks, False)
    expand(perm, incoming, taps, gains, nat, modes, chunks, False)
    field_grad = nat[...].astype(BF16).astype(F32)
    key_grad[...] = (field_grad * value[...].astype(F32)).astype(BF16)
    value_grad[...] = (field_grad * key[...].astype(F32)).astype(BF16)


def body(query, key, value, up, rates, freqs, residues, passthrough, norm_gain):
    tokens, width = query.shape
    modes = rates.shape[0]
    chunks = tokens // B
    blocks = width // LANES
    groups = lax.axis_size("ctx")
    me = lax.axis_index("ctx")

    def power(n):
        size = jnp.exp(-rates * n)
        return size * jnp.cos(freqs * n), size * jnp.sin(freqs * n)

    steps = jnp.arange(B + 1, dtype=F32)[None, :, None]
    size = jnp.exp(-rates[:, None, :] * steps)
    angle = freqs[:, None, :] * steps
    pow_re, pow_im = size * jnp.cos(angle), size * jnp.sin(angle)
    powers = jnp.concatenate([pow_re, pow_im], axis=1)
    weight = (residues * jnp.sqrt(rates))[:, None, :]
    gains = jnp.concatenate([weight * pow_re[:, :B], -weight * pow_im[:, :B]], axis=1)
    taps = jnp.sum(weight * pow_re[:, :B], axis=0)
    taps = taps.at[0].add(passthrough)
    jump = jnp.stack([pow_re[:, B], pow_im[:, B]])
    gain = norm_gain[None, :]

    def first_state(last, order):
        every = lax.all_gather(last, "ctx", axis=0)
        away = jnp.where(order > 0, order - 1, 0)[:, None, None].astype(F32) * tokens
        on = (order > 0)[:, None, None]
        size = jnp.where(on, jnp.exp(-rates[None] * away), 0.0)
        re, im = size * jnp.cos(freqs[None] * away), size * jnp.sin(freqs[None] * away)
        s_re, s_im = every[:, 0], every[:, 1]
        return jnp.stack(
            [jnp.sum(re * s_re - im * s_im, axis=0), jnp.sum(re * s_im + im * s_re, axis=0)]
        )

    place = jnp.arange(groups)
    tile = pl.BlockSpec((tokens, LANES), lambda i: (0, i))
    fixed = pl.BlockSpec((tokens, LANES), lambda i: (0, 0))
    row = pl.BlockSpec((1, LANES), lambda i: (0, i))
    pow_spec = pl.BlockSpec((modes, 2 * (B + 1), LANES), lambda i: (0, 0, i))
    gains_spec = pl.BlockSpec((modes, 2 * B, LANES), lambda i: (0, 0, i))
    taps_spec = pl.BlockSpec((B, LANES), lambda i: (0, i))
    pair = pl.BlockSpec((2, modes, LANES), lambda i: (0, 0, i))
    states_spec = pl.BlockSpec((2 * modes * chunks, LANES), lambda i: (0, i))
    field_shape = jax.ShapeDtypeStruct((tokens, width), BF16)
    sums_shape = jax.ShapeDtypeStruct((tokens, LANES), F32)
    states_shape = jax.ShapeDtypeStruct((2 * modes * chunks, width), F32)
    pair_shape = jax.ShapeDtypeStruct((2, modes, width), F32)
    scratch = [pltpu.VMEM((tokens, LANES), F32), pltpu.VMEM((tokens, LANES), F32)]
    incoming = pltpu.VMEM((2 * modes * chunks, LANES), F32)
    params = pltpu.CompilerParams(vmem_limit_bytes=48 * 1024 * 1024)

    def call(kernel, ins, outs, shapes, more, *args):
        return pl.pallas_call(
            functools.partial(kernel, modes, chunks),
            grid=(blocks,),
            in_specs=ins,
            out_specs=outs,
            out_shape=shapes,
            scratch_shapes=scratch + more,
            compiler_params=params,
        )(*args)

    states, last = call(
        forward_states_kernel,
        [tile, tile, pow_spec, pair],
        [states_spec, pair],
        [states_shape, pair_shape],
        [],
        key, value, powers, jump,
    )
    first = first_state(last, me - place)
    conv, squares, inners = call(
        forward_kernel,
        [tile, tile, tile, tile, row, states_spec, pair, pair, taps_spec, gains_spec],
        [tile, fixed, fixed],
        [field_shape, sums_shape, sums_shape],
        [incoming],
        key, value, query, up, gain, states, first, jump, taps, gains,
    )
    sums = lax.psum(jnp.stack([jnp.sum(squares, axis=1), jnp.sum(inners, axis=1)]), "tp")
    scale = lax.rsqrt(sums[0] / D + EPS)
    inner = sums[1] * scale / D
    scale_wide = jnp.broadcast_to(scale[:, None], (tokens, LANES))
    inner_wide = jnp.broadcast_to(inner[:, None], (tokens, LANES))
    output, query_grad, conv_grad, gain_part, states, last = call(
        middle_kernel,
        [tile, tile, tile, row, fixed, fixed, pow_spec, pair],
        [tile, tile, tile, row, states_spec, pair],
        [field_shape] * 3 + [jax.ShapeDtypeStruct((1, width), F32), states_shape, pair_shape],
        [],
        query, up, conv, gain, scale_wide, inner_wide, powers, jump,
    )
    gain_grad = lax.psum(gain_part[0], "ctx")
    first = first_state(last, place - me)
    key_grad, value_grad = call(
        backward_kernel,
        [tile, tile, tile, states_spec, pair, pair, taps_spec, gains_spec],
        [tile, tile],
        [field_shape] * 2,
        [incoming],
        conv_grad, key, value, states, first, jump, taps, gains,
    )
    return output, query_grad, key_grad, value_grad, gain_grad


def solution(mesh):
    field = P("ctx", "tp")
    return jax.shard_map(
        body,
        mesh=mesh,
        in_specs=(field,) * 4 + (P(None, "tp"),) * 3 + (P("tp"),) * 2,
        out_specs=(field,) * 4 + (P("tp"),),
        check_vma=False,
    )
```

```python
import functools

import jax
import jax.numpy as jnp
from jax import lax
from jax.experimental import pallas as pl
from jax.experimental.pallas import tpu as pltpu
from jax.sharding import PartitionSpec as P

D = 4096
EPS = 1e-06
B = 16
LANES = 128
SEGMENTS = 8
F32 = jnp.float32
BF16 = jnp.bfloat16


def token_rows(x, nat, perm, chunks):
    length = chunks * B
    for s in range(SEGMENTS):
        nat[pl.ds(s * (length + 8), length), :] = x[s * length : (s + 1) * length]
    for b in range(B):
        for a in range(chunks):
            perm[pl.ds((b * chunks + a) * SEGMENTS, SEGMENTS), :] = nat[
                pl.ds(a * B + b, SEGMENTS, stride=length + 8), :
            ]


def token_order(nat, chunks):
    length = chunks * B
    return jnp.concatenate(
        [nat[pl.ds(s * (length + 8), length), :] for s in range(SEGMENTS)], axis=0
    )


def product(a, b):
    return a[0] * b[0] - a[1] * b[1], a[0] * b[1] + a[1] * b[0]


def build_powers(root, powers, chunks):
    one = (root[0], root[1])
    powers[0] = jnp.ones_like(one[0])
    powers[B + 1] = jnp.zeros_like(one[0])
    now = one
    for b in range(1, B + 1):
        powers[b] = now[0]
        powers[B + 1 + b] = now[1]
        if b < B:
            now = product(now, one)
    far, count = None, chunks
    while count:
        if count & 1:
            far = now if far is None else product(far, now)
        count >>= 1
        if count:
            now = product(now, now)
    return far


def build_taps(powers, weight, skip, taps):
    for b in range(B):
        row = jnp.sum(weight[...] * powers[b], axis=0, keepdims=True)
        taps[b : b + 1, :] = row + skip[...] if b == 0 else row


def at(modes, part, m, per):
    return pl.multiple_of((part * modes + m) * per, 8)


def chunk_states(perm, powers, states, ends, modes, chunks, forward):
    count = chunks * SEGMENTS

    def step(i, carry):
        total = [[jnp.zeros((count, LANES), F32) for _ in range(2)] for _ in range(2)]
        for b in range(B):
            x = perm[pl.ds(b * count, count), :]
            k = B - b if forward else b + 1
            for j in range(2):
                m = 2 * i + j
                total[j][0] = total[j][0] + powers[k, pl.ds(m, 1), :] * x
                total[j][1] = total[j][1] + powers[B + 1 + k, pl.ds(m, 1), :] * x
        for j in range(2):
            m = 2 * i + j
            jump = (powers[B, pl.ds(m, 1), :], powers[2 * B + 1, pl.ds(m, 1), :])
            sums = None
            for a in range(chunks) if forward else reversed(range(chunks)):
                own = [total[j][p][a * SEGMENTS : (a + 1) * SEGMENTS] for p in range(2)]
                if sums is not None:
                    moved = product(jump, sums)
                    own = [own[0] + moved[0], own[1] + moved[1]]
                sums = own
            for part in range(2):
                states[pl.ds(at(modes, part, m, count), count), :] = total[j][part]
                ends[pl.ds(at(modes, part, m, SEGMENTS), SEGMENTS), :] = sums[part]
        return carry

    lax.fori_loop(0, modes // 2, step, 0)


def scan_segments(ends, now, far, out, modes, forward):
    for s in range(SEGMENTS) if forward else reversed(range(SEGMENTS)):
        rows = [pl.ds(part * modes * SEGMENTS + s, modes, stride=SEGMENTS) for part in range(2)]
        own = (ends[rows[0], :], ends[rows[1], :])
        if out is not None:
            out[rows[0], :] = now[0]
            out[rows[1], :] = now[1]
        moved = product(far, now)
        now = (moved[0] + own[0], moved[1] + own[1])
    return now


def scan_chunks(states, first, powers, weight, incoming, modes, chunks, forward):
    count = chunks * SEGMENTS

    def step(m, carry):
        jump = (powers[B, pl.ds(m, 1), :], powers[2 * B + 1, pl.ds(m, 1), :])
        scale = weight[pl.ds(m, 1), :]
        now = [first[pl.ds(at(modes, p, m, SEGMENTS), SEGMENTS), :] for p in range(2)]
        for a in range(chunks) if forward else reversed(range(chunks)):
            moved = product(jump, now)
            for p in range(2):
                rows = pl.ds(at(modes, p, m, count) + a * SEGMENTS, SEGMENTS)
                incoming[rows, :] = scale * now[p]
                now[p] = moved[p] + states[rows, :]
        return carry

    lax.fori_loop(0, modes, step, 0, unroll=2)


def expand(perm, incoming, taps, powers, nat, modes, chunks, forward):
    width = 8
    count = chunks * SEGMENTS
    pitch = chunks * B + 8
    part_rows = 2 * SEGMENTS

    for g in range(B // width):
        rows = [g * width + j for j in range(width)]

        def part(h, carry):
            base = pl.multiple_of(h * part_rows, part_rows)
            total = [None] * width
            for s in range(B):
                lags = [(t - s if forward else s - t) for t in rows]
                if max(lags) < 0:
                    continue
                x = perm[pl.ds(s * count + base, part_rows), :]
                for j, lag in enumerate(lags):
                    if lag >= 0:
                        term = taps[lag : lag + 1, :] * x
                        total[j] = term if total[j] is None else total[j] + term

            def step(i, sums):
                sums = list(sums)
                for n in range(4):
                    m = 4 * i + n
                    re = incoming[pl.ds(at(modes, 0, m, count) + base, part_rows), :]
                    im = incoming[pl.ds(at(modes, 1, m, count) + base, part_rows), :]
                    for j, t in enumerate(rows):
                        k = t if forward else B - 1 - t
                        sums[j] = (
                            sums[j]
                            + powers[k, pl.ds(m, 1), :] * re
                            - powers[B + 1 + k, pl.ds(m, 1), :] * im
                        )
                return tuple(sums)

            total = lax.fori_loop(0, modes // 4, step, tuple(total))
            for j, t in enumerate(rows):
                for e in range(2):
                    nat[pl.ds((2 * h + e) * B + t, SEGMENTS, stride=pitch), :] = total[j][
                        e * SEGMENTS : (e + 1) * SEGMENTS
                    ]
            return carry

        lax.fori_loop(0, chunks // 2, part, 0)


def forward_states_kernel(
    modes, chunks, key, value, root, states, ends, last, nat, perm, powers
):
    far = build_powers(root, powers, chunks)
    field = (key[...].astype(F32) * value[...].astype(F32)).astype(BF16).astype(F32)
    token_rows(field, nat, perm, chunks)
    chunk_states(perm, powers, states, ends, modes, chunks, True)
    zero = jnp.zeros((modes, LANES), F32)
    total = scan_segments(ends, (zero, zero), far, None, modes, True)
    last[0:modes, :] = total[0]
    last[modes:, :] = total[1]


def forward_kernel(
    modes, chunks, key, value, query, up, gain, states, ends, first, root, weight, skip,
    conv, squares, inners, nat, perm, powers, incoming, taps, starts,
):
    far = build_powers(root, powers, chunks)
    build_taps(powers, weight, skip, taps)
    field = (key[...].astype(F32) * value[...].astype(F32)).astype(BF16).astype(F32)
    token_rows(field, nat, perm, chunks)
    scan_segments(ends, (first[0], first[1]), far, starts, modes, True)
    scan_chunks(states, starts, powers, weight, incoming, modes, chunks, True)
    expand(perm, incoming, taps, powers, nat, modes, chunks, True)
    conv_out = token_order(nat, chunks).astype(BF16)
    conv[...] = conv_out
    gated = query[...].astype(F32) * conv_out.astype(F32)

    @pl.when(pl.program_id(0) == 0)
    def _():
        squares[...] = jnp.zeros_like(squares)
        inners[...] = jnp.zeros_like(inners)

    squares[...] += gated * gated
    inners[...] += up[...].astype(F32) * gain[...] * gated


def middle_kernel(
    modes, chunks, query, up, conv, gain, scale, inner, root,
    output, query_grad, conv_grad, states, ends, last, nat, perm, powers,
):
    q = query[...].astype(F32)
    c = conv[...].astype(F32)
    u = up[...].astype(F32)
    s = scale[...]
    normed = q * c * s
    output[...] = (normed * gain[...]).astype(BF16)
    gain_grad = jnp.sum(u * normed, axis=0, keepdims=True)
    grad_gated = s * (u * gain[...] - normed * inner[...])
    query_grad[...] = (grad_gated * c).astype(BF16)
    w = (grad_gated * q).astype(BF16)
    conv_grad[...] = w
    far = build_powers(root, powers, chunks)
    token_rows(w.astype(F32), nat, perm, chunks)
    chunk_states(perm, powers, states, ends, modes, chunks, False)
    zero = jnp.zeros((modes, LANES), F32)
    total = scan_segments(ends, (zero, zero), far, None, modes, False)
    last[0:modes, :] = total[0]
    last[modes : 2 * modes, :] = total[1]
    last[2 * modes :, :] = jnp.broadcast_to(gain_grad, (8, LANES))


def backward_kernel(
    modes, chunks, conv_grad, key, value, states, ends, first, root, weight, skip,
    key_grad, value_grad, nat, perm, powers, incoming, taps, starts,
):
    far = build_powers(root, powers, chunks)
    build_taps(powers, weight, skip, taps)
    token_rows(conv_grad[...].astype(F32), nat, perm, chunks)
    scan_segments(ends, (first[0], first[1]), far, starts, modes, False)
    scan_chunks(states, starts, powers, weight, incoming, modes, chunks, False)
    expand(perm, incoming, taps, powers, nat, modes, chunks, False)
    field_grad = token_order(nat, chunks).astype(BF16).astype(F32)
    key_grad[...] = (field_grad * value[...].astype(F32)).astype(BF16)
    value_grad[...] = (field_grad * key[...].astype(F32)).astype(BF16)


def body(query, key, value, up, rates, freqs, residues, passthrough, norm_gain):
    tokens, width = query.shape
    modes = rates.shape[0]
    chunks = tokens // (B * SEGMENTS)
    blocks = width // LANES
    groups = lax.axis_size("ctx")
    me = lax.axis_index("ctx")
    size = jnp.exp(-rates)
    root = jnp.stack([size * jnp.cos(freqs), size * jnp.sin(freqs)])
    weight = residues * jnp.sqrt(rates)
    skip = passthrough[None, :]
    gain = norm_gain[None, :]

    def first_state(every, order):
        away = jnp.where(order > 0, order - 1, 0)[:, None, None].astype(F32) * tokens
        on = (order > 0)[:, None, None]
        size = jnp.where(on, jnp.exp(-rates[None] * away), 0.0)
        re, im = size * jnp.cos(freqs[None] * away), size * jnp.sin(freqs[None] * away)
        s_re, s_im = every[:, :modes], every[:, modes : 2 * modes]
        return jnp.stack(
            [jnp.sum(re * s_re - im * s_im, axis=0), jnp.sum(re * s_im + im * s_re, axis=0)]
        )

    place = jnp.arange(groups)

    def columns(*rows):
        return pl.BlockSpec(rows + (LANES,), lambda i: (0,) * len(rows) + (i,))

    tile = columns(tokens)
    fixed = pl.BlockSpec((tokens, LANES), lambda i: (0, 0))
    row = columns(1)
    pair = columns(2, modes)
    mode = columns(modes)
    states_spec = columns(2 * modes * chunks * SEGMENTS)
    ends_spec = columns(2 * modes * SEGMENTS)
    field_shape = jax.ShapeDtypeStruct((tokens, width), BF16)
    sums_shape = jax.ShapeDtypeStruct((tokens, LANES), F32)

    def wide(rows):
        return jax.ShapeDtypeStruct((rows, width), F32)

    states_shape = wide(2 * modes * chunks * SEGMENTS)
    ends_shape = wide(2 * modes * SEGMENTS)
    scratch = [
        pltpu.VMEM((tokens + 8 * SEGMENTS, LANES), F32),
        pltpu.VMEM((tokens, LANES), F32),
        pltpu.VMEM((2 * (B + 1), modes, LANES), F32),
    ]
    more = [
        pltpu.VMEM((2 * modes * chunks * SEGMENTS, LANES), F32),
        pltpu.VMEM((B, LANES), F32),
        pltpu.VMEM((2 * modes * SEGMENTS, LANES), F32),
    ]
    params = pltpu.CompilerParams(vmem_limit_bytes=56 * 1024 * 1024)

    def call(kernel, ins, outs, shapes, more, *args):
        return pl.pallas_call(
            functools.partial(kernel, modes, chunks),
            grid=(blocks,),
            in_specs=ins,
            out_specs=outs,
            out_shape=shapes,
            scratch_shapes=scratch + more,
            compiler_params=params,
        )(*args)

    states, ends, last = call(
        forward_states_kernel,
        [tile, tile, pair],
        [states_spec, ends_spec, columns(2 * modes)],
        [states_shape, ends_shape, wide(2 * modes)],
        [],
        key, value, root,
    )
    first = first_state(lax.all_gather(last, "ctx", axis=0), me - place)
    conv, squares, inners = call(
        forward_kernel,
        [tile, tile, tile, tile, row, states_spec, ends_spec, pair, pair, mode, row],
        [tile, fixed, fixed],
        [field_shape, sums_shape, sums_shape],
        more,
        key, value, query, up, gain, states, ends, first, root, weight, skip,
    )
    sums = lax.psum(jnp.stack([jnp.sum(squares, axis=1), jnp.sum(inners, axis=1)]), "tp")
    scale = lax.rsqrt(sums[0] / D + EPS)
    inner = sums[1] * scale / D
    scale_wide = jnp.broadcast_to(scale[:, None], (tokens, LANES))
    inner_wide = jnp.broadcast_to(inner[:, None], (tokens, LANES))
    output, query_grad, conv_grad, states, ends, last = call(
        middle_kernel,
        [tile, tile, tile, row, fixed, fixed, pair],
        [tile, tile, tile, states_spec, ends_spec, columns(2 * modes + 8)],
        [field_shape] * 3 + [states_shape, ends_shape, wide(2 * modes + 8)],
        [],
        query, up, conv, gain, scale_wide, inner_wide, root,
    )
    every = lax.all_gather(last[: 2 * modes + 1], "ctx", axis=0)
    gain_grad = jnp.sum(every[:, 2 * modes], axis=0)
    first = first_state(every, place - me)
    key_grad, value_grad = call(
        backward_kernel,
        [tile, tile, tile, states_spec, ends_spec, pair, pair, mode, row],
        [tile, tile],
        [field_shape] * 2,
        more,
        conv_grad, key, value, states, ends, first, root, weight, skip,
    )
    return output, query_grad, key_grad, value_grad, gain_grad


def solution(mesh):
    field = P("ctx", "tp")
    return jax.shard_map(
        body,
        mesh=mesh,
        in_specs=(field,) * 4 + (P(None, "tp"),) * 3 + (P("tp"),) * 2,
        out_specs=(field,) * 4 + (P("tp"),),
        check_vma=False,
    )
```

```python
import functools

import jax
import jax.numpy as jnp
from jax import lax
from jax.experimental import pallas as pl
from jax.experimental.pallas import tpu as pltpu
from jax.sharding import PartitionSpec as P

D = 4096
EPS = 1e-06
B = 16
LANES = 128
SEGMENTS = 8
F32 = jnp.float32
BF16 = jnp.bfloat16


def token_rows(x, nat, perm, chunks):
    length = chunks * B
    for s in range(SEGMENTS):
        nat[pl.ds(s * (length + 8), length), :] = x[s * length : (s + 1) * length]
    for b in range(B):
        for a in range(chunks):
            perm[pl.ds((b * chunks + a) * SEGMENTS, SEGMENTS), :] = nat[
                pl.ds(a * B + b, SEGMENTS, stride=length + 8), :
            ]


def token_order(nat, chunks):
    length = chunks * B
    return jnp.concatenate(
        [nat[pl.ds(s * (length + 8), length), :] for s in range(SEGMENTS)], axis=0
    )


def product(a, b):
    return a[0] * b[0] - a[1] * b[1], a[0] * b[1] + a[1] * b[0]


def build_powers(root, powers, chunks):
    one = (root[0], root[1])
    powers[0] = jnp.ones_like(one[0])
    powers[B + 1] = jnp.zeros_like(one[0])
    now = one
    for b in range(1, B + 1):
        powers[b] = now[0]
        powers[B + 1 + b] = now[1]
        if b < B:
            now = product(now, one)
    far, count = None, chunks
    while count:
        if count & 1:
            far = now if far is None else product(far, now)
        count >>= 1
        if count:
            now = product(now, now)
    return far


def build_taps(powers, weight, skip, taps):
    for b in range(B):
        row = jnp.sum(weight[...] * powers[b], axis=0, keepdims=True)
        taps[b : b + 1, :] = row + skip[...] if b == 0 else row


def at(modes, part, m, per):
    return pl.multiple_of((part * modes + m) * per, 8)


def chunk_states(perm, powers, states, ends, modes, chunks, forward):
    count = chunks * SEGMENTS

    def step(i, carry):
        total = [[jnp.zeros((count, LANES), F32) for _ in range(2)] for _ in range(2)]
        for b in range(B):
            x = perm[pl.ds(b * count, count), :]
            k = B - b if forward else b + 1
            for j in range(2):
                m = 2 * i + j
                total[j][0] = total[j][0] + powers[k, pl.ds(m, 1), :] * x
                total[j][1] = total[j][1] + powers[B + 1 + k, pl.ds(m, 1), :] * x
        for j in range(2):
            m = 2 * i + j
            jump = (powers[B, pl.ds(m, 1), :], powers[2 * B + 1, pl.ds(m, 1), :])
            sums = None
            for a in range(chunks) if forward else reversed(range(chunks)):
                own = [total[j][p][a * SEGMENTS : (a + 1) * SEGMENTS] for p in range(2)]
                if sums is not None:
                    moved = product(jump, sums)
                    own = [own[0] + moved[0], own[1] + moved[1]]
                sums = own
            for part in range(2):
                states[pl.ds(at(modes, part, m, count), count), :] = total[j][part]
                ends[pl.ds(at(modes, part, m, SEGMENTS), SEGMENTS), :] = sums[part]
        return carry

    lax.fori_loop(0, modes // 2, step, 0)


def scan_segments(ends, now, far, out, modes, forward):
    for s in range(SEGMENTS) if forward else reversed(range(SEGMENTS)):
        rows = [pl.ds(part * modes * SEGMENTS + s, modes, stride=SEGMENTS) for part in range(2)]
        own = (ends[rows[0], :], ends[rows[1], :])
        if out is not None:
            out[rows[0], :] = now[0]
            out[rows[1], :] = now[1]
        moved = product(far, now)
        now = (moved[0] + own[0], moved[1] + own[1])
    return now


def scan_chunks(states, first, powers, weight, incoming, modes, chunks, forward):
    count = chunks * SEGMENTS

    def step(m, carry):
        jump = (powers[B, pl.ds(m, 1), :], powers[2 * B + 1, pl.ds(m, 1), :])
        scale = weight[pl.ds(m, 1), :]
        now = [first[pl.ds(at(modes, p, m, SEGMENTS), SEGMENTS), :] for p in range(2)]
        for a in range(chunks) if forward else reversed(range(chunks)):
            moved = product(jump, now)
            for p in range(2):
                rows = pl.ds(at(modes, p, m, count) + a * SEGMENTS, SEGMENTS)
                incoming[rows, :] = scale * now[p]
                now[p] = moved[p] + states[rows, :]
        return carry

    lax.fori_loop(0, modes, step, 0, unroll=2)


def expand(perm, incoming, taps, powers, nat, modes, chunks, forward):
    width = 8
    count = chunks * SEGMENTS
    pitch = chunks * B + 8
    part_rows = 2 * SEGMENTS

    for g in range(B // width):
        rows = [g * width + j for j in range(width)]

        def part(h, carry):
            base = pl.multiple_of(h * part_rows, part_rows)
            total = [None] * width
            for s in range(B):
                lags = [(t - s if forward else s - t) for t in rows]
                if max(lags) < 0:
                    continue
                x = perm[pl.ds(s * count + base, part_rows), :]
                for j, lag in enumerate(lags):
                    if lag >= 0:
                        term = taps[lag : lag + 1, :] * x
                        total[j] = term if total[j] is None else total[j] + term

            def step(i, sums):
                sums = list(sums)
                for n in range(4):
                    m = 4 * i + n
                    re = incoming[pl.ds(at(modes, 0, m, count) + base, part_rows), :]
                    im = incoming[pl.ds(at(modes, 1, m, count) + base, part_rows), :]
                    for j, t in enumerate(rows):
                        k = t if forward else B - 1 - t
                        sums[j] = (
                            sums[j]
                            + powers[k, pl.ds(m, 1), :] * re
                            - powers[B + 1 + k, pl.ds(m, 1), :] * im
                        )
                return tuple(sums)

            total = lax.fori_loop(0, modes // 4, step, tuple(total))
            for j, t in enumerate(rows):
                for e in range(2):
                    nat[pl.ds((2 * h + e) * B + t, SEGMENTS, stride=pitch), :] = total[j][
                        e * SEGMENTS : (e + 1) * SEGMENTS
                    ]
            return carry

        lax.fori_loop(0, chunks // 2, part, 0)


def forward_states_kernel(
    modes, chunks, key, value, root, states, ends, last, nat, perm, powers
):
    far = build_powers(root, powers, chunks)
    field = (key[...].astype(F32) * value[...].astype(F32)).astype(BF16).astype(F32)
    token_rows(field, nat, perm, chunks)
    chunk_states(perm, powers, states, ends, modes, chunks, True)
    zero = jnp.zeros((modes, LANES), F32)
    total = scan_segments(ends, (zero, zero), far, None, modes, True)
    last[0, 0:modes, :] = total[0]
    last[0, modes:, :] = total[1]


def forward_kernel(
    modes, chunks, key, value, query, up, gain, states, ends, first, root, weight, skip,
    conv, squares, inners, nat, perm, powers, incoming, taps, starts,
):
    far = build_powers(root, powers, chunks)
    build_taps(powers, weight, skip, taps)
    field = (key[...].astype(F32) * value[...].astype(F32)).astype(BF16).astype(F32)
    token_rows(field, nat, perm, chunks)
    scan_segments(ends, (first[0, 0:modes, :], first[0, modes : 2 * modes, :]), far, starts, modes, True)
    scan_chunks(states, starts, powers, weight, incoming, modes, chunks, True)
    expand(perm, incoming, taps, powers, nat, modes, chunks, True)
    conv_out = token_order(nat, chunks).astype(BF16)
    conv[...] = conv_out
    gated = query[...].astype(F32) * conv_out.astype(F32)

    @pl.when(pl.program_id(0) == 0)
    def _():
        squares[...] = jnp.zeros_like(squares)
        inners[...] = jnp.zeros_like(inners)

    squares[...] += gated * gated
    inners[...] += up[...].astype(F32) * gain[...] * gated


def middle_kernel(
    modes, chunks, query, up, conv, gain, scale, inner, root,
    output, query_grad, conv_grad, states, ends, last, nat, perm, powers,
):
    q = query[...].astype(F32)
    c = conv[...].astype(F32)
    u = up[...].astype(F32)
    s = scale[...]
    normed = q * c * s
    output[...] = (normed * gain[...]).astype(BF16)
    gain_grad = jnp.sum(u * normed, axis=0, keepdims=True)
    grad_gated = s * (u * gain[...] - normed * inner[...])
    query_grad[...] = (grad_gated * c).astype(BF16)
    w = (grad_gated * q).astype(BF16)
    conv_grad[...] = w
    far = build_powers(root, powers, chunks)
    token_rows(w.astype(F32), nat, perm, chunks)
    chunk_states(perm, powers, states, ends, modes, chunks, False)
    zero = jnp.zeros((modes, LANES), F32)
    total = scan_segments(ends, (zero, zero), far, None, modes, False)
    last[0, 0:modes, :] = total[0]
    last[0, modes : 2 * modes, :] = total[1]
    last[0, 2 * modes :, :] = jnp.broadcast_to(gain_grad, (16, LANES))


def backward_kernel(
    modes, chunks, conv_grad, key, value, states, ends, first, root, weight, skip,
    key_grad, value_grad, nat, perm, powers, incoming, taps, starts,
):
    far = build_powers(root, powers, chunks)
    build_taps(powers, weight, skip, taps)
    token_rows(conv_grad[...].astype(F32), nat, perm, chunks)
    scan_segments(ends, (first[0, 0:modes, :], first[0, modes : 2 * modes, :]), far, starts, modes, False)
    scan_chunks(states, starts, powers, weight, incoming, modes, chunks, False)
    expand(perm, incoming, taps, powers, nat, modes, chunks, False)
    field_grad = token_order(nat, chunks).astype(BF16).astype(F32)
    key_grad[...] = (field_grad * value[...].astype(F32)).astype(BF16)
    value_grad[...] = (field_grad * key[...].astype(F32)).astype(BF16)


def remote(source, target, send, receive, place):
    return pltpu.make_async_remote_copy(
        src_ref=source,
        dst_ref=target,
        send_sem=send,
        recv_sem=receive,
        device_id=place,
        device_id_type=pl.DeviceIdType.MESH,
    )


def turn(jump, state, modes):
    return product((jump[:modes], jump[modes:]), (state[:modes], state[modes : 2 * modes]))


def exchange_kernel(
    modes, groups, forward, last, jump, first, sibling_last, slots, own, other, sends, receives
):
    pairs = groups // 2
    me = lax.axis_index("ctx")
    side = lax.rem(me, 2)
    pair = me // 2
    sibling = me + 1 - 2 * side
    barrier = pltpu.get_barrier_semaphore()
    pl.semaphore_signal(
        barrier, inc=1, device_id={"ctx": sibling}, device_id_type=pl.DeviceIdType.MESH
    )
    for off in range(1, pairs):
        to = lax.rem(pair + off, pairs) * 2 + side
        pl.semaphore_signal(
            barrier, inc=1, device_id={"ctx": to}, device_id_type=pl.DeviceIdType.MESH
        )
    pl.semaphore_wait(barrier, pairs)

    copy = remote(last, sibling_last, sends.at[0], receives.at[0], {"ctx": sibling})
    copy.start()
    copy.wait()
    mine, theirs = last[side], sibling_last[side]
    leap = jump[side]
    late = side == (1 if forward else 0)
    farther = jnp.where(late, theirs, mine)
    nearer = jnp.where(late, mine, theirs)
    moved = turn(leap, farther, modes)
    joined = [moved[0] + nearer[:modes], moved[1] + nearer[modes : 2 * modes]]
    if last.shape[1] > 2 * modes:
        joined.append(mine[2 * modes :] + theirs[2 * modes :])
    slots[pair] = jnp.concatenate(joined, axis=0).astype(slots.dtype)

    copies = []
    for off in range(1, pairs):
        to = lax.rem(pair + off, pairs) * 2 + side
        copies.append(
            remote(slots.at[pair], slots.at[pair], sends.at[off], receives.at[off], {"ctx": to})
        )
    for copy in copies:
        copy.start()
    for copy in copies:
        copy.wait()
    twice = jnp.concatenate(product((leap[:modes], leap[modes:]), (leap[:modes], leap[modes:])))
    total = jnp.zeros((2 * modes, leap.shape[1]), F32)
    for p in range(pairs) if forward else reversed(range(pairs)):
        state = slots[p].astype(F32)
        moved = jnp.concatenate(turn(twice, total, modes), axis=0) + state[: 2 * modes]
        total = jnp.where(p < pair if forward else p > pair, moved, total)
    own[0 : 2 * modes, :] = total
    if last.shape[1] > 2 * modes:
        rest = slots[0, 2 * modes :, :].astype(F32)
        for p in range(1, pairs):
            rest = rest + slots[p, 2 * modes :, :].astype(F32)
        own[2 * modes :, :] = rest

    copy = remote(own, other, sends.at[pairs], receives.at[pairs], {"ctx": sibling})
    copy.start()
    copy.wait()
    for half in range(2):
        state = jnp.where(side == half, own[...], other[...])
        moved = jnp.concatenate(turn(jump[half], state, modes), axis=0)
        moved = moved + sibling_last[half, 0 : 2 * modes, :]
        first[half, 0 : 2 * modes, :] = jnp.where(late, moved, state[: 2 * modes])
        if last.shape[1] > 2 * modes:
            first[half, 2 * modes :, :] = state[2 * modes :]


def norm_kernel(peers, squares, inners, scale_wide, inner_wide, slots, sends, receives):
    me = lax.axis_index("tp")
    barrier = pltpu.get_barrier_semaphore()
    for off in range(1, peers):
        pl.semaphore_signal(
            barrier,
            inc=1,
            device_id={"tp": lax.rem(me + off, peers)},
            device_id_type=pl.DeviceIdType.MESH,
        )
    tokens = squares.shape[0]
    square_row = jnp.sum(squares[...].T, axis=0, keepdims=True)
    inner_row = jnp.sum(inners[...].T, axis=0, keepdims=True)
    upper = lax.broadcasted_iota(jnp.int32, (8, tokens), 0) < 4
    slots[me] = jnp.where(upper, square_row, inner_row)
    pl.semaphore_wait(barrier, peers - 1)
    copies = [
        remote(
            slots.at[me],
            slots.at[me],
            sends.at[off - 1],
            receives.at[off - 1],
            {"tp": lax.rem(me + off, peers)},
        )
        for off in range(1, peers)
    ]
    for copy in copies:
        copy.start()
    for copy in copies:
        copy.wait()
    total = slots[0]
    for p in range(1, peers):
        total = total + slots[p]
    scale = lax.rsqrt(total[0:1] / D + EPS)
    inner = total[4:5] * scale / D
    scale_wide[...] = jnp.broadcast_to(scale, (LANES, tokens)).T
    inner_wide[...] = jnp.broadcast_to(inner, (LANES, tokens)).T


def body(query, key, value, up, rates, freqs, residues, passthrough, norm_gain):
    tokens, width = query.shape
    modes = rates.shape[0]
    chunks = tokens // (B * SEGMENTS)
    blocks = width // LANES
    groups = lax.axis_size("ctx")
    size = jnp.exp(-rates)
    root = jnp.stack([size * jnp.cos(freqs), size * jnp.sin(freqs)])
    weight = residues * jnp.sqrt(rates)
    skip = passthrough[None, :]
    gain = norm_gain[None, :]

    half = width // 2
    turns = freqs * tokens
    size = jnp.exp(-rates * tokens)
    jump = jnp.concatenate([size * jnp.cos(turns), size * jnp.sin(turns)])
    jump = jump.reshape(2 * modes, 2, half).transpose(1, 0, 2)

    def exchange(last, forward):
        rows = last.shape[1]
        pairs = groups // 2
        return pl.pallas_call(
            functools.partial(exchange_kernel, modes, groups, forward),
            in_specs=[pl.BlockSpec(memory_space=pltpu.VMEM)] * 2,
            out_specs=pl.BlockSpec(memory_space=pltpu.VMEM),
            out_shape=jax.ShapeDtypeStruct((2, rows, half), F32),
            scratch_shapes=[
                pltpu.VMEM((2, rows, half), F32),
                pltpu.VMEM((pairs, rows, half), BF16),
                pltpu.VMEM((rows, half), F32),
                pltpu.VMEM((rows, half), F32),
                pltpu.SemaphoreType.DMA((pairs + 1,)),
                pltpu.SemaphoreType.DMA((pairs + 1,)),
            ],
            compiler_params=pltpu.CompilerParams(
                collective_id=0 if forward else 1, has_side_effects=True
            ),
        )(last, jump)

    def columns(*rows):
        return pl.BlockSpec(rows + (LANES,), lambda i: (0,) * len(rows) + (i,))

    tile = columns(tokens)
    fixed = pl.BlockSpec((tokens, LANES), lambda i: (0, 0))
    row = columns(1)
    pair = columns(2, modes)

    def halved(rows):
        per = blocks // 2
        return pl.BlockSpec((1, rows, LANES), lambda i: (i // per, 0, i % per))

    mode = columns(modes)
    states_spec = columns(2 * modes * chunks * SEGMENTS)
    ends_spec = columns(2 * modes * SEGMENTS)
    field_shape = jax.ShapeDtypeStruct((tokens, width), BF16)
    sums_shape = jax.ShapeDtypeStruct((tokens, LANES), F32)

    def wide(rows):
        return jax.ShapeDtypeStruct((rows, width), F32)

    states_shape = wide(2 * modes * chunks * SEGMENTS)
    ends_shape = wide(2 * modes * SEGMENTS)
    scratch = [
        pltpu.VMEM((tokens + 8 * SEGMENTS, LANES), F32),
        pltpu.VMEM((tokens, LANES), F32),
        pltpu.VMEM((2 * (B + 1), modes, LANES), F32),
    ]
    more = [
        pltpu.VMEM((2 * modes * chunks * SEGMENTS, LANES), F32),
        pltpu.VMEM((B, LANES), F32),
        pltpu.VMEM((2 * modes * SEGMENTS, LANES), F32),
    ]
    params = pltpu.CompilerParams(vmem_limit_bytes=56 * 1024 * 1024)

    def call(kernel, ins, outs, shapes, more, *args):
        return pl.pallas_call(
            functools.partial(kernel, modes, chunks),
            grid=(blocks,),
            in_specs=ins,
            out_specs=outs,
            out_shape=shapes,
            scratch_shapes=scratch + more,
            compiler_params=params,
        )(*args)

    states, ends, last = call(
        forward_states_kernel,
        [tile, tile, pair],
        [states_spec, ends_spec, halved(2 * modes)],
        [states_shape, ends_shape, jax.ShapeDtypeStruct((2, 2 * modes, half), F32)],
        [],
        key, value, root,
    )
    first = exchange(last, True)
    conv, squares, inners = call(
        forward_kernel,
        [tile, tile, tile, tile, row, states_spec, ends_spec, halved(2 * modes), pair, mode, row],
        [tile, fixed, fixed],
        [field_shape, sums_shape, sums_shape],
        more,
        key, value, query, up, gain, states, ends, first, root, weight, skip,
    )
    peers = lax.axis_size("tp")
    scale_wide, inner_wide = pl.pallas_call(
        functools.partial(norm_kernel, peers),
        in_specs=[pl.BlockSpec(memory_space=pltpu.VMEM)] * 2,
        out_specs=[pl.BlockSpec(memory_space=pltpu.VMEM)] * 2,
        out_shape=[sums_shape] * 2,
        scratch_shapes=[
            pltpu.VMEM((peers, 8, tokens), F32),
            pltpu.SemaphoreType.DMA((peers - 1,)),
            pltpu.SemaphoreType.DMA((peers - 1,)),
        ],
        compiler_params=pltpu.CompilerParams(collective_id=2, has_side_effects=True),
    )(squares, inners)
    output, query_grad, conv_grad, states, ends, last = call(
        middle_kernel,
        [tile, tile, tile, row, fixed, fixed, pair],
        [tile, tile, tile, states_spec, ends_spec, halved(2 * modes + 16)],
        [field_shape] * 3
        + [states_shape, ends_shape, jax.ShapeDtypeStruct((2, 2 * modes + 16, half), F32)],
        [],
        query, up, conv, gain, scale_wide, inner_wide, root,
    )
    first = exchange(last, False)
    gain_grad = first[:, 2 * modes].reshape(width)
    key_grad, value_grad = call(
        backward_kernel,
        [tile, tile, tile, states_spec, ends_spec, halved(2 * modes + 16), pair, mode, row],
        [tile, tile],
        [field_shape] * 2,
        more,
        conv_grad, key, value, states, ends, first, root, weight, skip,
    )
    return output, query_grad, key_grad, value_grad, gain_grad


def solution(mesh):
    field = P("ctx", "tp")
    return jax.shard_map(
        body,
        mesh=mesh,
        in_specs=(field,) * 4 + (P(None, "tp"),) * 3 + (P("tp"),) * 2,
        out_specs=(field,) * 4 + (P("tp"),),
        check_vma=False,
    )
```

```python
import functools

import jax
import jax.numpy as jnp
from jax import lax
from jax.experimental import pallas as pl
from jax.experimental.pallas import tpu as pltpu
from jax.sharding import PartitionSpec as P

D = 4096
EPS = 1e-06
B = 16
LANES = 128
SEGMENTS = 8
F32 = jnp.float32
BF16 = jnp.bfloat16


def token_rows(x, nat, perm, chunks):
    length = chunks * B
    for s in range(SEGMENTS):
        nat[pl.ds(s * (length + 8), length), :] = x[s * length : (s + 1) * length]
    for b in range(B):
        for a in range(chunks):
            perm[pl.ds((b * chunks + a) * SEGMENTS, SEGMENTS), :] = nat[
                pl.ds(a * B + b, SEGMENTS, stride=length + 8), :
            ]


def token_order(nat, chunks):
    length = chunks * B
    return jnp.concatenate(
        [nat[pl.ds(s * (length + 8), length), :] for s in range(SEGMENTS)], axis=0
    )


def product(a, b):
    return a[0] * b[0] - a[1] * b[1], a[0] * b[1] + a[1] * b[0]


def build_powers(root, powers, chunks):
    one = (root[0], root[1])
    powers[0] = jnp.ones_like(one[0])
    powers[B + 1] = jnp.zeros_like(one[0])
    now = one
    for b in range(1, B + 1):
        powers[b] = now[0]
        powers[B + 1 + b] = now[1]
        if b < B:
            now = product(now, one)
    far, count = None, chunks
    while count:
        if count & 1:
            far = now if far is None else product(far, now)
        count >>= 1
        if count:
            now = product(now, now)
    return far


def build_taps(powers, weight, skip, taps):
    for b in range(B):
        row = jnp.sum(weight[...] * powers[b], axis=0, keepdims=True)
        taps[b : b + 1, :] = row + skip[...] if b == 0 else row


def at(modes, part, m, per):
    return pl.multiple_of((part * modes + m) * per, 8)


def chunk_states(perm, powers, states, ends, modes, chunks, forward):
    count = chunks * SEGMENTS

    def step(i, carry):
        total = [[jnp.zeros((count, LANES), F32) for _ in range(2)] for _ in range(2)]
        for b in range(B):
            x = perm[pl.ds(b * count, count), :]
            k = B - b if forward else b + 1
            for j in range(2):
                m = 2 * i + j
                total[j][0] = total[j][0] + powers[k, pl.ds(m, 1), :] * x
                total[j][1] = total[j][1] + powers[B + 1 + k, pl.ds(m, 1), :] * x
        for j in range(2):
            m = 2 * i + j
            jump = (powers[B, pl.ds(m, 1), :], powers[2 * B + 1, pl.ds(m, 1), :])
            sums = None
            for a in range(chunks) if forward else reversed(range(chunks)):
                own = [total[j][p][a * SEGMENTS : (a + 1) * SEGMENTS] for p in range(2)]
                if sums is not None:
                    moved = product(jump, sums)
                    own = [own[0] + moved[0], own[1] + moved[1]]
                sums = own
            for part in range(2):
                states[pl.ds(at(modes, part, m, count), count), :] = total[j][part]
                ends[pl.ds(at(modes, part, m, SEGMENTS), SEGMENTS), :] = sums[part]
        return carry

    lax.fori_loop(0, modes // 2, step, 0)


def scan_segments(ends, now, far, out, modes, forward):
    for s in range(SEGMENTS) if forward else reversed(range(SEGMENTS)):
        rows = [pl.ds(part * modes * SEGMENTS + s, modes, stride=SEGMENTS) for part in range(2)]
        own = (ends[rows[0], :], ends[rows[1], :])
        if out is not None:
            out[rows[0], :] = now[0]
            out[rows[1], :] = now[1]
        moved = product(far, now)
        now = (moved[0] + own[0], moved[1] + own[1])
    return now


def scan_chunks(states, first, powers, weight, incoming, modes, chunks, forward):
    count = chunks * SEGMENTS

    def step(m, carry):
        jump = (powers[B, pl.ds(m, 1), :], powers[2 * B + 1, pl.ds(m, 1), :])
        scale = weight[pl.ds(m, 1), :]
        now = [first[pl.ds(at(modes, p, m, SEGMENTS), SEGMENTS), :] for p in range(2)]
        for a in range(chunks) if forward else reversed(range(chunks)):
            moved = product(jump, now)
            for p in range(2):
                rows = pl.ds(at(modes, p, m, count) + a * SEGMENTS, SEGMENTS)
                incoming[rows, :] = scale * now[p]
                now[p] = moved[p] + states[rows, :]
        return carry

    lax.fori_loop(0, modes, step, 0, unroll=2)


def expand(perm, incoming, taps, powers, nat, modes, chunks, forward):
    width = 8
    count = chunks * SEGMENTS
    pitch = chunks * B + 8
    part_rows = 2 * SEGMENTS

    for g in range(B // width):
        rows = [g * width + j for j in range(width)]

        def part(h, carry):
            base = pl.multiple_of(h * part_rows, part_rows)
            total = [None] * width
            for s in range(B):
                lags = [(t - s if forward else s - t) for t in rows]
                if max(lags) < 0:
                    continue
                x = perm[pl.ds(s * count + base, part_rows), :]
                for j, lag in enumerate(lags):
                    if lag >= 0:
                        term = taps[lag : lag + 1, :] * x
                        total[j] = term if total[j] is None else total[j] + term

            def step(i, sums):
                sums = list(sums)
                for n in range(4):
                    m = 4 * i + n
                    re = incoming[pl.ds(at(modes, 0, m, count) + base, part_rows), :]
                    im = incoming[pl.ds(at(modes, 1, m, count) + base, part_rows), :]
                    for j, t in enumerate(rows):
                        k = t if forward else B - 1 - t
                        sums[j] = (
                            sums[j]
                            + powers[k, pl.ds(m, 1), :] * re
                            - powers[B + 1 + k, pl.ds(m, 1), :] * im
                        )
                return tuple(sums)

            total = lax.fori_loop(0, modes // 4, step, tuple(total))
            for j, t in enumerate(rows):
                for e in range(2):
                    nat[pl.ds((2 * h + e) * B + t, SEGMENTS, stride=pitch), :] = total[j][
                        e * SEGMENTS : (e + 1) * SEGMENTS
                    ]
            return carry

        lax.fori_loop(0, chunks // 2, part, 0)


def forward_states_kernel(
    modes, chunks, key, value, root, states, ends, last, perm, nat, powers
):
    far = build_powers(root, powers, chunks)
    field = (key[...].astype(F32) * value[...].astype(F32)).astype(BF16).astype(F32)
    token_rows(field, nat, perm, chunks)
    chunk_states(perm, powers, states, ends, modes, chunks, True)
    zero = jnp.zeros((modes, LANES), F32)
    total = scan_segments(ends, (zero, zero), far, None, modes, True)
    last[0, 0:modes, :] = total[0]
    last[0, modes:, :] = total[1]


def forward_kernel(
    modes, chunks, perm, query, up, gain, states, ends, first, root, weight, skip,
    conv, squares, inners, nat, powers, incoming, taps, starts,
):
    far = build_powers(root, powers, chunks)
    build_taps(powers, weight, skip, taps)
    scan_segments(ends, (first[0, 0:modes, :], first[0, modes : 2 * modes, :]), far, starts, modes, True)
    scan_chunks(states, starts, powers, weight, incoming, modes, chunks, True)
    expand(perm, incoming, taps, powers, nat, modes, chunks, True)
    conv_out = token_order(nat, chunks).astype(BF16)
    conv[...] = conv_out
    gated = query[...].astype(F32) * conv_out.astype(F32)

    @pl.when(pl.program_id(0) == 0)
    def _():
        squares[...] = jnp.zeros_like(squares)
        inners[...] = jnp.zeros_like(inners)

    squares[...] += gated * gated
    inners[...] += up[...].astype(F32) * gain[...] * gated


def middle_kernel(
    modes, chunks, query, up, conv, gain, scale, inner, root,
    output, query_grad, states, ends, last, perm, nat, powers,
):
    q = query[...].astype(F32)
    c = conv[...].astype(F32)
    u = up[...].astype(F32)
    s = scale[...]
    normed = q * c * s
    output[...] = (normed * gain[...]).astype(BF16)
    gain_grad = jnp.sum(u * normed, axis=0, keepdims=True)
    grad_gated = s * (u * gain[...] - normed * inner[...])
    query_grad[...] = (grad_gated * c).astype(BF16)
    w = (grad_gated * q).astype(BF16)
    far = build_powers(root, powers, chunks)
    token_rows(w.astype(F32), nat, perm, chunks)
    chunk_states(perm, powers, states, ends, modes, chunks, False)
    zero = jnp.zeros((modes, LANES), F32)
    total = scan_segments(ends, (zero, zero), far, None, modes, False)
    last[0, 0:modes, :] = total[0]
    last[0, modes : 2 * modes, :] = total[1]
    last[0, 2 * modes :, :] = jnp.broadcast_to(gain_grad, (16, LANES))


def backward_kernel(
    modes, chunks, perm, key, value, states, ends, first, root, weight, skip,
    key_grad, value_grad, nat, powers, incoming, taps, starts,
):
    far = build_powers(root, powers, chunks)
    build_taps(powers, weight, skip, taps)
    scan_segments(ends, (first[0, 0:modes, :], first[0, modes : 2 * modes, :]), far, starts, modes, False)
    scan_chunks(states, starts, powers, weight, incoming, modes, chunks, False)
    expand(perm, incoming, taps, powers, nat, modes, chunks, False)
    field_grad = token_order(nat, chunks).astype(BF16).astype(F32)
    key_grad[...] = (field_grad * value[...].astype(F32)).astype(BF16)
    value_grad[...] = (field_grad * key[...].astype(F32)).astype(BF16)


def remote(source, target, send, receive, place):
    return pltpu.make_async_remote_copy(
        src_ref=source,
        dst_ref=target,
        send_sem=send,
        recv_sem=receive,
        device_id=place,
        device_id_type=pl.DeviceIdType.MESH,
    )


def turn(jump, state, modes):
    return product((jump[:modes], jump[modes:]), (state[:modes], state[modes : 2 * modes]))


def exchange_kernel(
    modes, groups, forward, last, jump, first, sibling_last, slots, own, other, sends, receives
):
    pairs = groups // 2
    me = lax.axis_index("ctx")
    side = lax.rem(me, 2)
    pair = me // 2
    sibling = me + 1 - 2 * side
    barrier = pltpu.get_barrier_semaphore()
    pl.semaphore_signal(
        barrier, inc=1, device_id={"ctx": sibling}, device_id_type=pl.DeviceIdType.MESH
    )
    for off in range(1, pairs):
        to = lax.rem(pair + off, pairs) * 2 + side
        pl.semaphore_signal(
            barrier, inc=1, device_id={"ctx": to}, device_id_type=pl.DeviceIdType.MESH
        )
    pl.semaphore_wait(barrier, pairs)

    copy = remote(last, sibling_last, sends.at[0], receives.at[0], {"ctx": sibling})
    copy.start()
    copy.wait()
    mine, theirs = last[side], sibling_last[side]
    leap = jump[side]
    late = side == (1 if forward else 0)
    farther = jnp.where(late, theirs, mine)
    nearer = jnp.where(late, mine, theirs)
    moved = turn(leap, farther, modes)
    joined = [moved[0] + nearer[:modes], moved[1] + nearer[modes : 2 * modes]]
    if last.shape[1] > 2 * modes:
        joined.append(mine[2 * modes :] + theirs[2 * modes :])
    slots[pair] = jnp.concatenate(joined, axis=0).astype(slots.dtype)

    copies = []
    for off in range(1, pairs):
        to = lax.rem(pair + off, pairs) * 2 + side
        copies.append(
            remote(slots.at[pair], slots.at[pair], sends.at[off], receives.at[off], {"ctx": to})
        )
    for copy in copies:
        copy.start()
    for copy in copies:
        copy.wait()
    twice = jnp.concatenate(product((leap[:modes], leap[modes:]), (leap[:modes], leap[modes:])))
    total = jnp.zeros((2 * modes, leap.shape[1]), F32)
    for p in range(pairs) if forward else reversed(range(pairs)):
        state = slots[p].astype(F32)
        moved = jnp.concatenate(turn(twice, total, modes), axis=0) + state[: 2 * modes]
        total = jnp.where(p < pair if forward else p > pair, moved, total)
    own[0 : 2 * modes, :] = total
    if last.shape[1] > 2 * modes:
        rest = slots[0, 2 * modes :, :].astype(F32)
        for p in range(1, pairs):
            rest = rest + slots[p, 2 * modes :, :].astype(F32)
        own[2 * modes :, :] = rest

    copy = remote(own, other, sends.at[pairs], receives.at[pairs], {"ctx": sibling})
    copy.start()
    copy.wait()
    for half in range(2):
        state = jnp.where(side == half, own[...], other[...])
        moved = jnp.concatenate(turn(jump[half], state, modes), axis=0)
        moved = moved + sibling_last[half, 0 : 2 * modes, :]
        first[half, 0 : 2 * modes, :] = jnp.where(late, moved, state[: 2 * modes])
        if last.shape[1] > 2 * modes:
            first[half, 2 * modes :, :] = state[2 * modes :]


def norm_kernel(peers, squares, inners, scale_wide, inner_wide, slots, sends, receives):
    me = lax.axis_index("tp")
    barrier = pltpu.get_barrier_semaphore()
    for off in range(1, peers):
        pl.semaphore_signal(
            barrier,
            inc=1,
            device_id={"tp": lax.rem(me + off, peers)},
            device_id_type=pl.DeviceIdType.MESH,
        )
    tokens = squares.shape[0]
    square_row = jnp.sum(squares[...].T, axis=0, keepdims=True)
    inner_row = jnp.sum(inners[...].T, axis=0, keepdims=True)
    upper = lax.broadcasted_iota(jnp.int32, (8, tokens), 0) < 4
    slots[me] = jnp.where(upper, square_row, inner_row)
    pl.semaphore_wait(barrier, peers - 1)
    copies = [
        remote(
            slots.at[me],
            slots.at[me],
            sends.at[off - 1],
            receives.at[off - 1],
            {"tp": lax.rem(me + off, peers)},
        )
        for off in range(1, peers)
    ]
    for copy in copies:
        copy.start()
    for copy in copies:
        copy.wait()
    total = slots[0]
    for p in range(1, peers):
        total = total + slots[p]
    scale = lax.rsqrt(total[0:1] / D + EPS)
    inner = total[4:5] * scale / D
    scale_wide[...] = jnp.broadcast_to(scale, (LANES, tokens)).T
    inner_wide[...] = jnp.broadcast_to(inner, (LANES, tokens)).T


def body(query, key, value, up, rates, freqs, residues, passthrough, norm_gain):
    tokens, width = query.shape
    modes = rates.shape[0]
    chunks = tokens // (B * SEGMENTS)
    blocks = width // LANES
    groups = lax.axis_size("ctx")
    size = jnp.exp(-rates)
    root = jnp.stack([size * jnp.cos(freqs), size * jnp.sin(freqs)])
    weight = residues * jnp.sqrt(rates)
    skip = passthrough[None, :]
    gain = norm_gain[None, :]

    half = width // 2
    turns = freqs * tokens
    size = jnp.exp(-rates * tokens)
    jump = jnp.concatenate([size * jnp.cos(turns), size * jnp.sin(turns)])
    jump = jump.reshape(2 * modes, 2, half).transpose(1, 0, 2)

    def exchange(last, forward):
        rows = last.shape[1]
        pairs = groups // 2
        return pl.pallas_call(
            functools.partial(exchange_kernel, modes, groups, forward),
            in_specs=[pl.BlockSpec(memory_space=pltpu.VMEM)] * 2,
            out_specs=pl.BlockSpec(memory_space=pltpu.VMEM),
            out_shape=jax.ShapeDtypeStruct((2, rows, half), F32),
            scratch_shapes=[
                pltpu.VMEM((2, rows, half), F32),
                pltpu.VMEM((pairs, rows, half), BF16),
                pltpu.VMEM((rows, half), F32),
                pltpu.VMEM((rows, half), F32),
                pltpu.SemaphoreType.DMA((pairs + 1,)),
                pltpu.SemaphoreType.DMA((pairs + 1,)),
            ],
            compiler_params=pltpu.CompilerParams(
                collective_id=0 if forward else 1, has_side_effects=True
            ),
        )(last, jump)

    def columns(*rows):
        return pl.BlockSpec(rows + (LANES,), lambda i: (0,) * len(rows) + (i,))

    tile = columns(tokens)
    fixed = pl.BlockSpec((tokens, LANES), lambda i: (0, 0))
    row = columns(1)
    pair = columns(2, modes)

    def halved(rows):
        per = blocks // 2
        return pl.BlockSpec((1, rows, LANES), lambda i: (i // per, 0, i % per))

    mode = columns(modes)
    states_spec = columns(2 * modes * chunks * SEGMENTS)
    ends_spec = columns(2 * modes * SEGMENTS)
    field_shape = jax.ShapeDtypeStruct((tokens, width), BF16)
    sums_shape = jax.ShapeDtypeStruct((tokens, LANES), F32)

    def wide(rows):
        return jax.ShapeDtypeStruct((rows, width), F32)

    states_shape = wide(2 * modes * chunks * SEGMENTS)
    ends_shape = wide(2 * modes * SEGMENTS)
    scratch = [
        pltpu.VMEM((tokens + 8 * SEGMENTS, LANES), F32),
        pltpu.VMEM((2 * (B + 1), modes, LANES), F32),
    ]
    more = [
        pltpu.VMEM((2 * modes * chunks * SEGMENTS, LANES), F32),
        pltpu.VMEM((B, LANES), F32),
        pltpu.VMEM((2 * modes * SEGMENTS, LANES), F32),
    ]
    params = pltpu.CompilerParams(vmem_limit_bytes=56 * 1024 * 1024)

    def call(kernel, ins, outs, shapes, more, *args):
        return pl.pallas_call(
            functools.partial(kernel, modes, chunks),
            grid=(blocks,),
            in_specs=ins,
            out_specs=outs,
            out_shape=shapes,
            scratch_shapes=scratch + more,
            compiler_params=params,
        )(*args)

    states, ends, last, perm = call(
        forward_states_kernel,
        [tile, tile, pair],
        [states_spec, ends_spec, halved(2 * modes), tile],
        [states_shape, ends_shape, jax.ShapeDtypeStruct((2, 2 * modes, half), F32), wide(tokens)],
        [],
        key, value, root,
    )
    first = exchange(last, True)
    conv, squares, inners = call(
        forward_kernel,
        [tile, tile, tile, row, states_spec, ends_spec, halved(2 * modes), pair, mode, row],
        [tile, fixed, fixed],
        [field_shape, sums_shape, sums_shape],
        more,
        perm, query, up, gain, states, ends, first, root, weight, skip,
    )
    peers = lax.axis_size("tp")
    scale_wide, inner_wide = pl.pallas_call(
        functools.partial(norm_kernel, peers),
        in_specs=[pl.BlockSpec(memory_space=pltpu.VMEM)] * 2,
        out_specs=[pl.BlockSpec(memory_space=pltpu.VMEM)] * 2,
        out_shape=[sums_shape] * 2,
        scratch_shapes=[
            pltpu.VMEM((peers, 8, tokens), F32),
            pltpu.SemaphoreType.DMA((peers - 1,)),
            pltpu.SemaphoreType.DMA((peers - 1,)),
        ],
        compiler_params=pltpu.CompilerParams(collective_id=2, has_side_effects=True),
    )(squares, inners)
    output, query_grad, states, ends, last, perm = call(
        middle_kernel,
        [tile, tile, tile, row, fixed, fixed, pair],
        [tile, tile, states_spec, ends_spec, halved(2 * modes + 16), tile],
        [field_shape] * 2
        + [states_shape, ends_shape, jax.ShapeDtypeStruct((2, 2 * modes + 16, half), F32)]
        + [wide(tokens)],
        [],
        query, up, conv, gain, scale_wide, inner_wide, root,
    )
    first = exchange(last, False)
    gain_grad = first[:, 2 * modes].reshape(width)
    key_grad, value_grad = call(
        backward_kernel,
        [tile, tile, tile, states_spec, ends_spec, halved(2 * modes + 16), pair, mode, row],
        [tile, tile],
        [field_shape] * 2,
        more,
        perm, key, value, states, ends, first, root, weight, skip,
    )
    return output, query_grad, key_grad, value_grad, gain_grad


def solution(mesh):
    field = P("ctx", "tp")
    return jax.shard_map(
        body,
        mesh=mesh,
        in_specs=(field,) * 4 + (P(None, "tp"),) * 3 + (P("tp"),) * 2,
        out_specs=(field,) * 4 + (P("tp"),),
        check_vma=False,
    )
```
